512 devices in a mesh: cam: 8 (over y, x_lo), seq: 64 (over z, x_hi, core).
Axes of the slice: x: 4 (x_hi: 2, x_lo: 2; x = x_hi * 2 + x_lo), y: 4, z: 16, core: 2. Of those that a mesh axis runs over, the one named last changes fastest.
Arguments:
- query: bfloat16 [8, 384, 64, 1536], P('cam', 'seq'), may hold values from -5 to 5
- key: bfloat16 [8, 384, 64, 1536], P('cam', 'seq'), may hold values from -5 to 5
- value: bfloat16 [8, 384, 64, 1536], P('cam', 'seq'), may hold values from -6 to 6
- edge_cols: int32 [8], replicated, may hold values from 2 to 14, as said below
Outputs:
- mixed: bfloat16 [8, 384, 64, 1536], P('cam', 'seq')
The draws below stay inside these ranges and needn't reach their ends.
Inputs may be any that keep to these rules, and one draw needn't show every extreme that they name: `edge_cols`: at least one pair has exactly 14 shared columns.
All inputs are finite; a program needn't handle non-finite values.
Results may differ from the reference program's by a relative error of at most 0.0045.
Values may be sent and summed in bfloat16 or wider, within the bound.
A program may use at most 128 MiB of HBM per device.

```python
import jax
import jax.numpy as jnp
from jax import lax

HD = 128
ROWS = 12
COLS = 32
MAX_COLS = 14
WIDTH = 1536
FT = 384
FRAMES = 64
CAMS = 8


def draw_query(key, part):
    key = jax.random.fold_in(key, 1)
    shape = (CAMS, FT, FRAMES, WIDTH)
    base = jnp.clip(jax.random.normal(key, shape, jnp.float32), -5.0, 5.0)
    return base.astype(jnp.bfloat16)


def draw_key(key, part):
    key = jax.random.fold_in(key, 2)
    shape = (CAMS, FT, FRAMES, WIDTH)
    base = jnp.clip(jax.random.normal(key, shape, jnp.float32), -5.0, 5.0)
    return base.astype(jnp.bfloat16)


def draw_edge_cols(key, part):
    key = jax.random.fold_in(key, 3)
    widths = jax.random.randint(key, (CAMS,), 2, MAX_COLS + 1)
    chosen = jax.random.randint(jax.random.fold_in(key, 4), (), 0, CAMS)
    slots = lax.iota(jnp.int32, CAMS)
    return jnp.where(slots == chosen, MAX_COLS, widths).astype(jnp.int32)


def level_of(own_key, dims, split, smallest, top_value):
    def one(axis_at, parts):
        draws = jax.random.uniform(jax.random.fold_in(jax.random.fold_in(own_key, 6), axis_at), (parts,), jnp.float32, smallest / len(split), top_value / len(split))
        return jnp.repeat(jnp.exp(draws), dims[axis_at] // parts).reshape((-1,) + (1,) * (len(dims) - axis_at - 1))

    loudness = one(*split[0])
    for cut in split[1:]:
        loudness = loudness * one(*cut)
    return loudness


def bell_draw(rng, dims, deviation, bound, shards=(), kind=jnp.bfloat16):
    gain = level_of(rng, dims, shards, -0.22, 0.18) if shards else 1.0
    values = jax.random.normal(rng, dims, jnp.float32) * deviation * gain
    return jnp.minimum(jnp.maximum(values, -bound), bound).astype(kind)


def setup_inputs(seed: int = 0) -> dict:
    key_of = jax.random.split(jax.random.key(seed), 5)
    return {
        "query": draw_query(jax.random.fold_in(key_of[4], 71), 0),
        "key": draw_key(jax.random.fold_in(key_of[4], 71), 0),
        "value": bell_draw(key_of[2], (CAMS, FT, FRAMES, WIDTH), 1.0, 6.0, ((0, 8), (1, 64))),
        "edge_cols": draw_edge_cols(jax.random.fold_in(key_of[4], 71), 0),
    }


def attend(query_rows, key_rows, value_rows, valid):
    count = query_rows.shape[0]
    frames = query_rows.shape[1]
    heads = query_rows.shape[2] // HD
    q_four = query_rows.astype(jnp.float32).reshape(count, frames, heads, HD)
    k_four = key_rows.astype(jnp.float32).reshape(key_rows.shape[0], frames, heads, HD)
    v_four = value_rows.astype(jnp.float32).reshape(value_rows.shape[0], frames, heads, HD)
    scores = jnp.einsum('qfhd,kfhd->fhqk', q_four, k_four) * (HD ** -0.5)
    if valid is not None:
        scores = jnp.where(valid[None, None, None, :], scores, -1e30)
    top = jnp.max(scores, axis=-1, keepdims=True)
    expo = jnp.exp(scores - top)
    weights = (expo / jnp.sum(expo, axis=-1, keepdims=True)).astype(jnp.bfloat16)
    weights = lax.optimization_barrier(weights).astype(jnp.float32)
    result = jnp.einsum('fhqk,kfhd->qfhd', weights, v_four)
    return result.reshape(count, frames, heads * HD)


def blocks(whole):
    cams, frames, width = whole.shape[0], whole.shape[2], whole.shape[3]
    grid = whole.reshape(cams, ROWS, COLS, frames, width)
    left = grid[:, :, :MAX_COLS].reshape(cams, ROWS * MAX_COLS, frames, width)
    right = grid[:, :, COLS - MAX_COLS:].reshape(cams, ROWS * MAX_COLS, frames, width)
    return left, right


def reference(query, key, value, edge_cols):
    q_left, q_right = blocks(query)
    k_left, k_right = blocks(key)
    v_left, v_right = blocks(value)
    column = jnp.tile(jnp.arange(MAX_COLS, dtype=jnp.int32), ROWS)
    edge = ROWS * MAX_COLS

    def pair(item):
        a_q, a_k, a_v, b_q, b_k, b_v, shared = item
        valid = jnp.concatenate([column >= MAX_COLS - shared, column < shared])
        joint = attend(jnp.concatenate([a_q, b_q]), jnp.concatenate([a_k, b_k]),
                       jnp.concatenate([a_v, b_v]), valid)
        joint = joint * valid[:, None, None].astype(jnp.float32)
        return joint[:edge], joint[edge:]

    right_out, next_left = lax.map(pair, (q_right, k_right, v_right,
                                          jnp.roll(q_left, -1, 0), jnp.roll(k_left, -1, 0),
                                          jnp.roll(v_left, -1, 0), edge_cols))
    left_out = jnp.roll(next_left, 1, 0)

    def camera(item):
        q_cam, k_cam, v_cam, left_part, right_part = item
        frames, width = q_cam.shape[1], q_cam.shape[2]

        def frame(pieces):
            q_one, k_one, v_one = pieces
            return attend(q_one[:, None], k_one[:, None], v_one[:, None], None)[:, 0]

        spatial = lax.map(frame, (q_cam.transpose(1, 0, 2), k_cam.transpose(1, 0, 2), v_cam.transpose(1, 0, 2)))
        total = spatial.transpose(1, 0, 2).reshape(ROWS, COLS, frames, width)
        total = total.at[:, :MAX_COLS].add(left_part.reshape(ROWS, MAX_COLS, frames, width))
        total = total.at[:, COLS - MAX_COLS:].add(right_part.reshape(ROWS, MAX_COLS, frames, width))
        return total.reshape(ROWS * COLS, frames, width).astype(jnp.bfloat16)

    return lax.map(camera, (query, key, value, left_out, right_out))
```

```python
import jax
import jax.numpy as jnp
from jax import lax
from jax.experimental import pallas as pl
from jax.experimental.pallas import tpu as pltpu
from jax.sharding import PartitionSpec as P

MESH = pl.DeviceIdType.MESH
HD = 128
COLS = 32
MAX_COLS = 14
BF = jnp.bfloat16
F32 = jnp.float32
NZ = 16
NG = 4
BLK = 6
FR = 16
HEADS = 3
FG = 4
PER = 4
POS = NZ * BLK
EDGE = 48
MID = 16
ROWS_G = 2 * EDGE + MID
AHEAD = 2
SCALE = HD**-0.5 * 1.4426950408889634


def tables():
    slots, cols, counts = [], [], []
    for g in range(NG):
        left, right, mid = [], [], []
        for b in range(PER):
            for i in range(BLK):
                col = (PER * BLK * b + BLK * g + i) % COLS
                entry = (BLK * b + i, col)
                (left if col < MAX_COLS else right if col >= COLS - MAX_COLS else mid).append(entry)
        groups = [left, right, mid]
        counts.append([len(x) for x in groups])
        row_s, row_c = [], []
        for x, room in zip(groups, (EDGE // 4, EDGE // 4, MID // 4)):
            for k in range(room):
                row_s.append(x[k][0] if k < len(x) else x[0][0])
                row_c.append(x[k][1] if k < len(x) else -1)
        slots.append(row_s)
        cols.append(row_c)
    return slots, cols, counts


SLOTS, COLUMNS, COUNTS = tables()
KINDS = len(SLOTS[0])


def by_g(g, values):
    if len(set(values)) == 1:
        return values[0]
    out = jnp.int32(values[-1])
    for n in range(len(values) - 2, -1, -1):
        out = jnp.where(g == n, jnp.int32(values[n]), out)
    return out


def dot(a, b, dims):
    return lax.dot_general(a, b, (dims, ((), ())), preferred_element_type=F32)


def kernel(
    edge_ref, q_ref, k_ref, v_ref, out_ref,
    rxz, st2, rx2, edges, ost, rxo, otx, perm, ones, bias, qvalid,
    z_send, z_recv, g_send, g_recv, e_send, e_recv, og_send, og_recv, oz_send, oz_recv,
):
    cam = lax.axis_index("cam")
    seq = lax.axis_index("seq")
    cams = lax.axis_size("cam")
    z = seq // NG
    g = seq % NG
    prior = lax.rem(cam + cams - 1, cams)
    after = lax.rem(cam + 1, cams)
    hg, fg = z // 4, z % 4
    args = (k_ref, v_ref, q_ref)

    def ring(d):
        return lax.rem(z + d, NZ)

    bar = pltpu.get_barrier_semaphore()

    def greet(dev):
        pl.semaphore_signal(bar, inc=1, device_id=dev, device_id_type=MESH)

    @pl.loop(1, NZ)
    def _(d):
        greet((cam, ring(d) * NG + g))

    for d in range(1, NG):
        greet((cam, z * NG + lax.rem(g + d, NG)))
    for d in range(NG):
        greet((prior, z * NG + d))
        greet((after, z * NG + d))
    pl.semaphore_wait(bar, NZ - 1 + NG - 1 + 2 * NG)

    def z_src(t, h, zt):
        rows = pl.ds(pl.multiple_of((zt % 4) * FR, FR), FR)
        lanes = pl.ds(pl.multiple_of(((zt // 4) * HEADS + h) * HD, HD), HD)
        return args[t].at[:, rows, lanes]

    def z_issue(t, h):
        dst = rxz.at[t, h, pl.ds(z * BLK, BLK)]

        def go(d):
            zt = ring(d)
            pltpu.make_async_remote_copy(
                z_src(t, h, zt), dst, z_send.at[t, h], z_recv.at[t, h],
                device_id=(cam, zt * NG + g), device_id_type=MESH,
            ).start()

        @pl.loop(1, NZ // 2)
        def _(d):
            go(d)
            go(NZ - d)

        go(NZ // 2)
        pltpu.make_async_copy(z_src(t, h, z), dst, z_recv.at[t, h]).start()

    def wait_bytes(ref, sem):
        pltpu.make_async_copy(ref, ref, sem).wait()

    z_issue(0, 0)
    z_issue(1, 0)

    r = lax.broadcasted_iota(jnp.int32, (256, 256), 0)
    c = lax.broadcasted_iota(jnp.int32, (256, 256), 1)
    hit = c == (r % 16) * 16 + r // 16
    perm[0] = jnp.where(hit, 1.0, 0.0).astype(BF)
    perm[1] = jnp.where(jnp.logical_and(hit, r % 16 < 8), 1.0, 0.0).astype(BF)

    def column_of(idx, kind):
        dev, k = idx // EDGE, (idx % EDGE) // 4
        col = jnp.full(idx.shape, -1, jnp.int32)
        for n in range(NG):
            for kk in range(COUNTS[n][kind]):
                here = jnp.logical_and(dev == n, k == kk)
                col = jnp.where(here, COLUMNS[n][kind * (EDGE // 4) + kk], col)
        return col

    w_right = edge_ref[cam]
    w_left = edge_ref[prior]

    def on_left(col, w):
        return jnp.logical_and(col >= 0, col < w)

    def on_right(col, w):
        return col >= COLS - w

    lane = lax.broadcasted_iota(jnp.int32, (8, NG * EDGE), 1)
    col_l, col_r = column_of(lane, 0), column_of(lane, 1)

    def as_bias(ok):
        return jnp.where(ok, 0.0, -1e30).astype(F32)

    bias[0] = jnp.concatenate([as_bias(on_right(col_r, w_left)), as_bias(on_left(col_l, w_left))], axis=1)
    bias[1] = jnp.concatenate([as_bias(on_right(col_r, w_right)), as_bias(on_left(col_l, w_right))], axis=1)
    row = lax.broadcasted_iota(jnp.int32, (NG * EDGE, HD), 0)
    qvalid[0] = jnp.where(on_left(column_of(row, 0), w_left), 1.0, 0.0).astype(F32)
    qvalid[1] = jnp.where(on_right(column_of(row, 1), w_right), 1.0, 0.0).astype(F32)
    for n in range(NG):
        for kind, (base, room) in enumerate(((0, EDGE), (NG * EDGE, EDGE), (2 * NG * EDGE, MID))):
            at = lax.broadcasted_iota(jnp.int32, (room, HD), 0)
            ones[base + n * room : base + (n + 1) * room] = jnp.where(at < 4 * COUNTS[n][kind], 1.0, 0.0).astype(BF)

    slot = [by_g(g, [SLOTS[n][k] for n in range(NG)]) for k in range(KINDS)]
    room_of = [(0, k) for k in range(EDGE // 4)] + [(1, k) for k in range(EDGE // 4)] + [(2, k) for k in range(MID // 4)]
    real = [by_g(g, [1 if k < COUNTS[n][kind] else 0 for n in range(NG)]) for kind, k in room_of]

    def place(k, a):
        if isinstance(real[k], int):
            return PER * BLK * a + slot[k]
        return jnp.where(real[k] == 1, PER * BLK * a + slot[k], POS)

    def to_frames(t, h, zero_pads):
        for j in range(KINDS // 4):
            tiles = []
            for k in range(4 * j, 4 * j + 4):
                for a in range(4):
                    tiles.append(rxz[t, h, PER * BLK * a + slot[k]])
            x = jnp.concatenate(tiles, axis=0)
            last = real[4 * j + 3]
            which = 0 if (isinstance(last, int) or not zero_pads) else 1 - last
            y = dot(perm[which], x, ((1,), (0,)))
            st2[t, h, :, 16 * j : 16 * j + 16, :] = y.astype(BF).reshape(FR, 16, HD)

    def to_tiles(h):
        for j in range(KINDS // 4):
            x = rxo[h, :, 16 * j : 16 * j + 16, :].reshape(256, HD)
            y = dot(perm[0], x, ((1,), (0,))).astype(BF).reshape(16, FR, HD)
            for n in range(16):
                otx[h, place(4 * j + n // 4, n % 4)] = y[n]

    def g_issue(t, h, with_edges):
        for d in (2, 1, 3):
            gt = lax.rem(g + d, NG)
            pltpu.make_async_remote_copy(
                st2.at[t, h, pl.ds(gt * FG, FG)], rx2.at[t, h, g], g_send.at[t, h], g_recv.at[t, h],
                device_id=(cam, z * NG + gt), device_id_type=MESH,
            ).start()
        pltpu.make_async_copy(st2.at[t, h, pl.ds(g * FG, FG)], rx2.at[t, h, g], g_recv.at[t, h]).start()
        if with_edges:
            for d in range(NG):
                gt = lax.rem(g + d, NG)
                for side, who, base in ((0, after, EDGE), (1, prior, 0)):
                    pltpu.make_async_remote_copy(
                        st2.at[t, h, pl.ds(gt * FG, FG), pl.ds(base, EDGE)], edges.at[t, h, side, g],
                        e_send.at[t, h], e_recv.at[t, h],
                        device_id=(who, z * NG + gt), device_id_type=MESH,
                    ).start()

    def arrive(t, h, zero_pads, with_edges):
        wait_bytes(rxz.at[t, h], z_recv.at[t, h])
        nt = (t + AHEAD) % 3
        if t + AHEAD < 3:
            z_issue(nt, h)
        else:
            @pl.when(h < HEADS - 1)
            def _():
                z_issue(nt, h + 1)
        to_frames(t, h, zero_pads)
        g_issue(t, h, with_edges)

    def weigh(q, k, v, extra):
        s = dot(q, k, ((1,), (1,))) * SCALE
        if extra is not None:
            s = s + extra
        p = jnp.exp2(s - jnp.max(s, axis=-1, keepdims=True)).astype(BF)
        acc = dot(p, v, ((1,), (0,)))
        return acc[:, :HD] / acc[:, HD:]

    def gather(t, h, f, lo, n):
        return jnp.concatenate([rx2[t, h, gs, f, lo : lo + n, :] for gs in range(NG)], axis=0)

    def edge(t, h, f, side):
        return jnp.concatenate([edges[t, h, side, gs, f] for gs in range(NG)], axis=0)

    def attend(h):
        for t in range(3):
            wait_bytes(rx2.at[t, h], g_recv.at[t, h])
        for t in range(2):
            wait_bytes(edges.at[t, h], e_recv.at[t, h])

        @pl.loop(0, FG)
        def _(f):
            kl, kr, km = gather(0, h, f, 0, EDGE), gather(0, h, f, EDGE, EDGE), gather(0, h, f, 2 * EDGE, MID)
            vl, vr, vm = gather(1, h, f, 0, EDGE), gather(1, h, f, EDGE, EDGE), gather(1, h, f, 2 * EDGE, MID)
            ql, qr, qm = gather(2, h, f, 0, EDGE), gather(2, h, f, EDGE, EDGE), gather(2, h, f, 2 * EDGE, MID)
            k_all = jnp.concatenate([kl, kr, km], axis=0)
            v_all = jnp.concatenate([jnp.concatenate([vl, vr, vm], axis=0), ones[...]], axis=1)
            full = jnp.full((2 * NG * EDGE, HD), 1.0, BF)
            k_left = jnp.concatenate([edge(0, h, f, 0), kl], axis=0)
            v_left = jnp.concatenate([jnp.concatenate([edge(1, h, f, 0), vl], axis=0), full], axis=1)
            k_right = jnp.concatenate([kr, edge(0, h, f, 1)], axis=0)
            v_right = jnp.concatenate([jnp.concatenate([vr, edge(1, h, f, 1)], axis=0), full], axis=1)
            o_l = weigh(ql, k_all, v_all, None) + weigh(ql, k_left, v_left, bias[0, 0:1]) * qvalid[0]
            o_r = weigh(qr, k_all, v_all, None) + weigh(qr, k_right, v_right, bias[1, 0:1]) * qvalid[1]
            o_m = weigh(qm, k_all, v_all, None)
            o_l, o_r, o_m = o_l.astype(BF), o_r.astype(BF), o_m.astype(BF)
            for n in range(NG):
                ost[h, n, f, 0:EDGE, :] = o_l[n * EDGE : (n + 1) * EDGE]
                ost[h, n, f, EDGE : 2 * EDGE, :] = o_r[n * EDGE : (n + 1) * EDGE]
                ost[h, n, f, 2 * EDGE :, :] = o_m[n * MID : (n + 1) * MID]
            for d in (2, 1, 3):
                gt = lax.rem(g + d, NG)
                pltpu.make_async_remote_copy(
                    ost.at[h, gt, f], rxo.at[h, g * FG + f], og_send.at[h], og_recv.at[h],
                    device_id=(cam, z * NG + gt), device_id_type=MESH,
                ).start()
            pltpu.make_async_copy(ost.at[h, g, f], rxo.at[h, g * FG + f], og_recv.at[h]).start()

    def give_back(h):
        wait_bytes(rxo.at[h], og_recv.at[h])
        to_tiles(h)
        dst = out_ref.at[:, pl.ds(pl.multiple_of(fg * FR, FR), FR), pl.ds(pl.multiple_of((hg * HEADS + h) * HD, HD), HD)]

        def go(d):
            zt = ring(d)
            pltpu.make_async_remote_copy(
                otx.at[h, pl.ds(zt * BLK, BLK)], dst, oz_send.at[h], oz_recv.at[h],
                device_id=(cam, zt * NG + g), device_id_type=MESH,
            ).start()

        @pl.loop(1, NZ // 2)
        def _(d):
            go(d)
            go(NZ - d)

        go(NZ // 2)
        pltpu.make_async_copy(otx.at[h, pl.ds(z * BLK, BLK)], dst, oz_recv.at[h]).start()

    @pl.loop(0, HEADS)
    def _(h):
        arrive(0, h, False, True)

        @pl.when(h > 0)
        def _():
            attend(h - 1)

        arrive(1, h, True, True)

        @pl.when(h == HEADS - 1)
        def _():
            @pl.loop(0, HEADS - 1)
            def _(hh):
                give_back(hh)

        arrive(2, h, False, False)

    attend(HEADS - 1)
    give_back(HEADS - 1)

    @pl.loop(0, HEADS)
    def _(h):
        for t in range(3):
            wait_bytes(rxz.at[t, h, pl.ds(0, (NZ - 1) * BLK)], z_send.at[t, h])
            wait_bytes(rx2.at[t, h, pl.ds(0, NG - 1)], g_send.at[t, h])
        for t in range(2):
            wait_bytes(edges.at[t, h], e_send.at[t, h])
        wait_bytes(rx2.at[0, h, pl.ds(0, NG - 1)], og_send.at[h])
        wait_bytes(rxz.at[0, h, pl.ds(0, (NZ - 1) * BLK)], oz_send.at[h])
        wait_bytes(rxz.at[0, h], oz_recv.at[h])


def local(query, key, value, edge_cols):
    dma = pltpu.SemaphoreType.DMA
    out = pl.pallas_call(
        kernel,
        out_shape=jax.ShapeDtypeStruct(query.shape[1:], query.dtype),
        in_specs=[pl.BlockSpec(memory_space=pltpu.SMEM)] + [pl.BlockSpec(memory_space=pl.ANY)] * 3,
        out_specs=pl.BlockSpec(memory_space=pl.ANY),
        scratch_shapes=[
            pltpu.VMEM((3, HEADS, POS, FR, HD), BF),
            pltpu.VMEM((3, HEADS, FR, ROWS_G, HD), BF),
            pltpu.VMEM((3, HEADS, NG, FG, ROWS_G, HD), BF),
            pltpu.VMEM((2, HEADS, 2, NG, FG, EDGE, HD), BF),
            pltpu.VMEM((HEADS, NG, FG, ROWS_G, HD), BF),
            pltpu.VMEM((HEADS, FR, ROWS_G, HD), BF),
            pltpu.VMEM((HEADS, POS + 1, FR, HD), BF),
            pltpu.VMEM((2, 256, 256), BF),
            pltpu.VMEM((NG * ROWS_G, HD), BF),
            pltpu.VMEM((2, 8, 2 * NG * EDGE), F32),
            pltpu.VMEM((2, NG * EDGE, HD), F32),
            dma((3, HEADS)), dma((3, HEADS)), dma((3, HEADS)), dma((3, HEADS)), dma((2, HEADS)), dma((2, HEADS)),
            dma((HEADS,)), dma((HEADS,)), dma((HEADS,)), dma((HEADS,)),
        ],
        compiler_params=pltpu.CompilerParams(collective_id=0, has_side_effects=True, vmem_limit_bytes=56 * 2**20),
    )(edge_cols, query[0], key[0], value[0])
    return out[None]


def solution(mesh):
    spec = P("cam", "seq", None, None)
    return jax.shard_map(local, mesh=mesh, in_specs=(spec, spec, spec, P()), out_specs=spec, check_vma=False)
```

```python
import jax
import jax.numpy as jnp
from jax import lax
from jax.experimental import pallas as pl
from jax.experimental.pallas import tpu as pltpu
from jax.sharding import PartitionSpec as P

MESH = pl.DeviceIdType.MESH
HD = 128
COLS = 32
MAX_COLS = 14
BF = jnp.bfloat16
F32 = jnp.float32
NZ = 16
NG = 4
BLK = 6
FR = 16
HEADS = 3
FG = 4
PER = 4
POS = NZ * BLK
EDGE = 48
MID = 16
ROWS_G = 2 * EDGE + MID
ROOMS = (EDGE, EDGE, MID)
SETS = ((0, 2), (2, 1))
AHEAD = 2
SCALE = HD**-0.5 * 1.4426950408889634


def tables():
    slots, cols, counts = [], [], []
    for g in range(NG):
        left, right, mid = [], [], []
        for b in range(PER):
            for i in range(BLK):
                col = (PER * BLK * b + BLK * g + i) % COLS
                entry = (BLK * b + i, col)
                (left if col < MAX_COLS else right if col >= COLS - MAX_COLS else mid).append(entry)
        groups = [left, right, mid]
        counts.append([len(x) for x in groups])
        row_s, row_c = [], []
        for x, room in zip(groups, [room // 4 for room in ROOMS]):
            for k in range(room):
                row_s.append(x[k][0] if k < len(x) else x[0][0])
                row_c.append(x[k][1] if k < len(x) else -1)
        slots.append(row_s)
        cols.append(row_c)
    return slots, cols, counts


SLOTS, COLUMNS, COUNTS = tables()
KINDS = len(SLOTS[0])


def by_g(g, values):
    if len(set(values)) == 1:
        return values[0]
    out = jnp.int32(values[-1])
    for n in range(len(values) - 2, -1, -1):
        out = jnp.where(g == n, jnp.int32(values[n]), out)
    return out


def dot(a, b, dims):
    return lax.dot_general(a, b, (dims, ((), ())), preferred_element_type=F32)


def kernel(
    edge_ref, q_ref, k_ref, v_ref, out_ref,
    rxz_a, st2_a, rx2_a, edges_a, ost_a, rxo_a, otx_a,
    rxz_b, st2_b, rx2_b, edges_b, ost_b, rxo_b, otx_b,
    perm, bias, qvalid,
    z_send, z_recv, g_send, g_recv, e_send, e_recv, og_send, og_recv, oz_send, oz_recv,
):
    cam = lax.axis_index("cam")
    seq = lax.axis_index("seq")
    cams = lax.axis_size("cam")
    z = seq // NG
    g = seq % NG
    prior = lax.rem(cam + cams - 1, cams)
    after = lax.rem(cam + 1, cams)
    hg, fg = z // 4, z % 4
    args = (k_ref, v_ref, q_ref)
    rxz, st2, rx2, edges = (rxz_a, rxz_b), (st2_a, st2_b), (rx2_a, rx2_b), (edges_a, edges_b)
    ost, rxo, otx = (ost_a, ost_b), (rxo_a, rxo_b), (otx_a, otx_b)

    def ring(d):
        return lax.rem(z + d, NZ)

    bar = pltpu.get_barrier_semaphore()

    def greet(dev):
        pl.semaphore_signal(bar, inc=1, device_id=dev, device_id_type=MESH)

    @pl.loop(1, NZ)
    def _(d):
        greet((cam, ring(d) * NG + g))

    for d in range(1, NG):
        greet((cam, z * NG + lax.rem(g + d, NG)))
    for d in range(NG):
        greet((prior, z * NG + d))
        greet((after, z * NG + d))
    pl.semaphore_wait(bar, NZ - 1 + NG - 1 + 2 * NG)

    def lanes_of(zt, s):
        first, count = SETS[s]
        return pl.ds(pl.multiple_of(((zt // 4) * HEADS + first) * HD, HD), count * HD)

    def frames_of(zt):
        return pl.ds(pl.multiple_of((zt % 4) * FR, FR), FR)

    def to_ring(go):
        @pl.loop(1, NZ // 2)
        def _(d):
            go(ring(d))
            go(ring(NZ - d))

        go(ring(NZ // 2))

    def z_issue(chunk):
        s, t = chunk
        dst = rxz[s].at[t, pl.ds(z * BLK, BLK)]

        def src(zt):
            return args[t].at[:, frames_of(zt), lanes_of(zt, s)]

        def go(zt):
            pltpu.make_async_remote_copy(
                src(zt), dst, z_send.at[s, t], z_recv.at[s, t], device_id=(cam, zt * NG + g), device_id_type=MESH
            ).start()

        to_ring(go)
        pltpu.make_async_copy(src(z), dst, z_recv.at[s, t]).start()

    def wait_bytes(ref, sem):
        pltpu.make_async_copy(ref, ref, sem).wait()

    chunks = [(s, t) for s in range(len(SETS)) for t in range(3)]
    for chunk in chunks[:AHEAD]:
        z_issue(chunk)

    r = lax.broadcasted_iota(jnp.int32, (256, 256), 0)
    c = lax.broadcasted_iota(jnp.int32, (256, 256), 1)
    perm[...] = jnp.where(c == (r % 16) * 16 + r // 16, 1.0, 0.0).astype(BF)

    def column_of(idx, kind):
        room = ROOMS[kind]
        dev, k = idx // room, (idx % room) // 4
        col = jnp.full(idx.shape, -1, jnp.int32)
        for n in range(NG):
            for kk in range(COUNTS[n][kind]):
                here = jnp.logical_and(dev == n, k == kk)
                col = jnp.where(here, COLUMNS[n][sum(ROOMS[:kind]) // 4 + kk], col)
        return col

    w_right = edge_ref[cam]
    w_left = edge_ref[prior]

    def on_left(col, w):
        return jnp.logical_and(col >= 0, col < w)

    def on_right(col, w):
        return col >= COLS - w

    lane = lax.broadcasted_iota(jnp.int32, (8, NG * EDGE), 1)
    col_l, col_r = column_of(lane, 0), column_of(lane, 1)
    col_m = column_of(lax.broadcasted_iota(jnp.int32, (8, NG * MID), 1), 2)

    def as_bias(*ok):
        return jnp.concatenate([jnp.where(x, 0.0, -1e30).astype(F32) for x in ok], axis=1)

    bias[0] = as_bias(col_l >= 0, col_r >= 0, col_m >= 0)
    bias[1, :, : 2 * NG * EDGE] = as_bias(on_right(col_r, w_left), on_left(col_l, w_left))
    bias[2, :, : 2 * NG * EDGE] = as_bias(on_right(col_r, w_right), on_left(col_l, w_right))
    row = lax.broadcasted_iota(jnp.int32, (NG * EDGE, HD), 0)
    qvalid[0] = jnp.where(on_left(column_of(row, 0), w_left), 1.0, 0.0).astype(F32)
    qvalid[1] = jnp.where(on_right(column_of(row, 1), w_right), 1.0, 0.0).astype(F32)

    slot = [by_g(g, [SLOTS[n][k] for n in range(NG)]) for k in range(KINDS)]
    kinds = [(kind, k) for kind in range(3) for k in range(ROOMS[kind] // 4)]
    real = [by_g(g, [1 if k < COUNTS[n][kind] else 0 for n in range(NG)]) for kind, k in kinds]

    def place(k, a):
        if isinstance(real[k], int):
            return PER * BLK * a + slot[k]
        return jnp.where(real[k] == 1, PER * BLK * a + slot[k], POS)

    def to_frames(s, t):
        for j in range(KINDS // 4):
            x = jnp.concatenate(
                [rxz[s][t, PER * BLK * a + slot[k]] for k in range(4 * j, 4 * j + 4) for a in range(4)], axis=0
            )
            y = dot(perm[...], x, ((1,), (0,))).astype(BF)
            st2[s][t, :, 16 * j : 16 * j + 16, :] = y.reshape(FR, 16, x.shape[1])

    def to_tiles(s):
        for j in range(KINDS // 4):
            x = rxo[s][:, 16 * j : 16 * j + 16, :]
            x = x.reshape(256, x.shape[2])
            y = dot(perm[...], x, ((1,), (0,))).astype(BF).reshape(16, FR, x.shape[1])
            for n in range(16):
                otx[s][place(4 * j + n // 4, n % 4)] = y[n]

    def g_issue(s, t):
        for d in (2, 1, 3):
            gt = lax.rem(g + d, NG)
            pltpu.make_async_remote_copy(
                st2[s].at[t, pl.ds(gt * FG, FG)], rx2[s].at[t, g], g_send.at[s, t], g_recv.at[s, t],
                device_id=(cam, z * NG + gt), device_id_type=MESH,
            ).start()
        pltpu.make_async_copy(st2[s].at[t, pl.ds(g * FG, FG)], rx2[s].at[t, g], g_recv.at[s, t]).start()
        if t < 2:
            for d in range(NG):
                gt = lax.rem(g + d, NG)
                for side, who, base in ((0, after, EDGE), (1, prior, 0)):
                    pltpu.make_async_remote_copy(
                        st2[s].at[t, pl.ds(gt * FG, FG), pl.ds(base, EDGE)], edges[s].at[t, side, g],
                        e_send.at[s, t], e_recv.at[s, t],
                        device_id=(who, z * NG + gt), device_id_type=MESH,
                    ).start()

    def arrive(n):
        s, t = chunks[n]
        wait_bytes(rxz[s].at[t], z_recv.at[s, t])
        if n + AHEAD < len(chunks):
            z_issue(chunks[n + AHEAD])
        to_frames(s, t)
        g_issue(s, t)

    def weigh(q, k, v, extra):
        x = dot(q, k, ((1,), (1,))) * SCALE + extra
        p = jnp.exp2(x - jnp.max(x, axis=-1, keepdims=True))
        w = (p * (1.0 / jnp.sum(p, axis=-1, keepdims=True))).astype(BF)
        return dot(w, v, ((1,), (0,)))

    def attend(s):
        for t in range(3):
            wait_bytes(rx2[s].at[t], g_recv.at[s, t])
        for t in range(2):
            wait_bytes(edges[s].at[t], e_recv.at[s, t])
        count = SETS[s][1]

        @pl.loop(0, FG * count)
        def _(n):
            f, h = n // count, n % count
            lanes = pl.ds(pl.multiple_of(h * HD, HD), HD)

            def gather(t):
                parts, lo = [], 0
                for room in ROOMS:
                    parts.append([rx2[s][t, gs, f, lo : lo + room, lanes] for gs in range(NG)])
                    lo += room
                return [jnp.concatenate(x, axis=0) for x in parts]

            def edge(t, side):
                return jnp.concatenate([edges[s][t, side, gs, f, :, lanes] for gs in range(NG)], axis=0)

            (kl, kr, km), (vl, vr, vm), (ql, qr, qm) = gather(0), gather(1), gather(2)
            k_all, v_all = jnp.concatenate([kl, kr, km], axis=0), jnp.concatenate([vl, vr, vm], axis=0)
            k_left, v_left = jnp.concatenate([edge(0, 0), kl], axis=0), jnp.concatenate([edge(1, 0), vl], axis=0)
            k_right, v_right = jnp.concatenate([kr, edge(0, 1)], axis=0), jnp.concatenate([vr, edge(1, 1)], axis=0)
            here, joint_l, joint_r = bias[0, 0:1], bias[1, 0:1, : 2 * NG * EDGE], bias[2, 0:1, : 2 * NG * EDGE]
            o_l = weigh(ql, k_all, v_all, here) + weigh(ql, k_left, v_left, joint_l) * qvalid[0]
            o_r = weigh(qr, k_all, v_all, here) + weigh(qr, k_right, v_right, joint_r) * qvalid[1]
            o_m = weigh(qm, k_all, v_all, here)
            o_l, o_r, o_m = o_l.astype(BF), o_r.astype(BF), o_m.astype(BF)
            for gs in range(NG):
                ost[s][gs, f, 0:EDGE, lanes] = o_l[gs * EDGE : (gs + 1) * EDGE]
                ost[s][gs, f, EDGE : 2 * EDGE, lanes] = o_r[gs * EDGE : (gs + 1) * EDGE]
                ost[s][gs, f, 2 * EDGE :, lanes] = o_m[gs * MID : (gs + 1) * MID]
            for d in (2, 1, 3):
                gt = lax.rem(g + d, NG)
                pltpu.make_async_remote_copy(
                    ost[s].at[gt, f, :, lanes], rxo[s].at[g * FG + f, :, lanes], og_send.at[s], og_recv.at[s],
                    device_id=(cam, z * NG + gt), device_id_type=MESH,
                ).start()
            pltpu.make_async_copy(
                ost[s].at[g, f, :, lanes], rxo[s].at[g * FG + f, :, lanes], og_recv.at[s]
            ).start()

    def give_back(s):
        wait_bytes(rxo[s], og_recv.at[s])
        to_tiles(s)
        dst = out_ref.at[:, frames_of(z), lanes_of(z, s)]

        def go(zt):
            pltpu.make_async_remote_copy(
                otx[s].at[pl.ds(zt * BLK, BLK)], dst, oz_send.at[s], oz_recv.at[s],
                device_id=(cam, zt * NG + g), device_id_type=MESH,
            ).start()

        to_ring(go)
        pltpu.make_async_copy(otx[s].at[pl.ds(z * BLK, BLK)], dst, oz_recv.at[s]).start()

    arrive(0)
    arrive(1)
    arrive(2)
    arrive(3)
    attend(0)
    arrive(4)
    give_back(0)
    arrive(5)
    attend(1)
    give_back(1)

    for s in range(len(SETS)):
        for t in range(3):
            wait_bytes(rxz[s].at[t, pl.ds(0, (NZ - 1) * BLK)], z_send.at[s, t])
            wait_bytes(rx2[s].at[t, pl.ds(0, NG - 1)], g_send.at[s, t])
        for t in range(2):
            wait_bytes(edges[s].at[t], e_send.at[s, t])
        wait_bytes(ost[s].at[pl.ds(0, NG - 1)], og_send.at[s])
        wait_bytes(rxz[s].at[0, pl.ds(0, (NZ - 1) * BLK)], oz_send.at[s])
        wait_bytes(rxz[s].at[0], oz_recv.at[s])


def local(query, key, value, edge_cols):
    sems = [(2, 3)] * 4 + [(2, 2)] * 2 + [(2,)] * 4
    buffers = []
    for _, count in SETS:
        wide = count * HD
        for shape in (
            (3, POS, FR), (3, FR, ROWS_G), (3, NG, FG, ROWS_G), (2, 2, NG, FG, EDGE), (NG, FG, ROWS_G), (FR, ROWS_G), (POS + 1, FR)
        ):
            buffers.append(pltpu.VMEM(shape + (wide,), BF))
    out = pl.pallas_call(
        kernel,
        out_shape=jax.ShapeDtypeStruct(query.shape[1:], query.dtype),
        in_specs=[pl.BlockSpec(memory_space=pltpu.SMEM)] + [pl.BlockSpec(memory_space=pl.ANY)] * 3,
        out_specs=pl.BlockSpec(memory_space=pl.ANY),
        scratch_shapes=buffers
        + [pltpu.VMEM((256, 256), BF), pltpu.VMEM((3, 8, NG * ROWS_G), F32), pltpu.VMEM((2, NG * EDGE, HD), F32)]
        + [pltpu.SemaphoreType.DMA(shape) for shape in sems],
        compiler_params=pltpu.CompilerParams(collective_id=0, has_side_effects=True, vmem_limit_bytes=52 * 2**20),
    )(edge_cols, query[0], key[0], value[0])
    return out[None]


def solution(mesh):
    spec = P("cam", "seq", None, None)
    return jax.shard_map(local, mesh=mesh, in_specs=(spec, spec, spec, P()), out_specs=spec, check_vma=False)
```

```python
import jax
import jax.numpy as jnp
from jax import lax
from jax.experimental import pallas as pl
from jax.experimental.pallas import tpu as pltpu
from jax.sharding import PartitionSpec as P

MESH = pl.DeviceIdType.MESH
HD = 128
COLS = 32
MAX_COLS = 14
BF = jnp.bfloat16
F32 = jnp.float32
NZ = 16
NG = 4
BLK = 6
FR = 16
HEADS = 3
FG = 4
PER = 4
POS = NZ * BLK
EDGE = 48
MID = 16
ROWS_G = 2 * EDGE + MID
ROOMS = (EDGE, EDGE, MID)
SETS = ((0, 2), (2, 1))
AHEAD = 2
FIRST = 4
SCALE = HD**-0.5 * 1.4426950408889634


def tables():
    slots, cols, counts = [], [], []
    for g in range(NG):
        left, right, mid = [], [], []
        for b in range(PER):
            for i in range(BLK):
                col = (PER * BLK * b + BLK * g + i) % COLS
                entry = (BLK * b + i, col)
                (left if col < MAX_COLS else right if col >= COLS - MAX_COLS else mid).append(entry)
        groups = [left, right, mid]
        counts.append([len(x) for x in groups])
        row_s, row_c = [], []
        for x, room in zip(groups, [room // 4 for room in ROOMS]):
            for k in range(room):
                row_s.append(x[k][0] if k < len(x) else x[0][0])
                row_c.append(x[k][1] if k < len(x) else -1)
        slots.append(row_s)
        cols.append(row_c)
    return slots, cols, counts


SLOTS, COLUMNS, COUNTS = tables()
KINDS = len(SLOTS[0])


def by_g(g, values):
    if len(set(values)) == 1:
        return values[0]
    out = jnp.int32(values[-1])
    for n in range(len(values) - 2, -1, -1):
        out = jnp.where(g == n, jnp.int32(values[n]), out)
    return out


def dot(a, b, dims):
    return lax.dot_general(a, b, (dims, ((), ())), preferred_element_type=F32)


def kernel(
    edge_ref, q_ref, k_ref, v_ref, out_ref,
    rxz_a, st2_a, rx2_a, edges_a, ost_a, rxo_a, otx_a,
    rxz_b, st2_b, rx2_b, edges_b, ost_b, rxo_b, otx_b,
    perm, bias, qvalid,
    z_send, z_recv, g_send, g_recv, e_send, e_recv, og_send, og_recv, oz_send, oz_recv,
):
    cam = lax.axis_index("cam")
    seq = lax.axis_index("seq")
    cams = lax.axis_size("cam")
    z = seq // NG
    g = seq % NG
    prior = lax.rem(cam + cams - 1, cams)
    after = lax.rem(cam + 1, cams)
    hg, fg = z // 4, z % 4
    args = (k_ref, v_ref, q_ref)
    rxz, st2, rx2, edges = (rxz_a, rxz_b), (st2_a, st2_b), (rx2_a, rx2_b), (edges_a, edges_b)
    ost, rxo, otx = (ost_a, ost_b), (rxo_a, rxo_b), (otx_a, otx_b)

    def ring(d):
        return lax.rem(z + d, NZ)

    bar = pltpu.get_barrier_semaphore()

    def greet(dev):
        pl.semaphore_signal(bar, inc=1, device_id=dev, device_id_type=MESH)

    @pl.loop(1, NZ)
    def _(d):
        greet((cam, ring(d) * NG + g))

    for d in range(1, NG):
        greet((cam, z * NG + lax.rem(g + d, NG)))
    for d in range(NG):
        greet((prior, z * NG + d))
        greet((after, z * NG + d))
    pl.semaphore_wait(bar, NZ - 1 + NG - 1 + 2 * NG)

    def lanes_of(zt, s):
        first, count = SETS[s]
        return pl.ds(pl.multiple_of(((zt // 4) * HEADS + first) * HD, HD), count * HD)

    def frames_of(zt):
        return pl.ds(pl.multiple_of((zt % 4) * FR, FR), FR)

    def to_ring(go):
        @pl.loop(1, NZ // 2)
        def _(d):
            go(ring(d))
            go(ring(NZ - d))

        go(ring(NZ // 2))

    def back_to_ring(go):
        def go_if(ok, zt):
            pl.when(ok)(lambda: go(zt))

        @pl.loop(1, NZ // 2)
        def _(d):
            zt = lax.rem(z + d, FIRST)
            go_if(jnp.logical_and(d <= FIRST, zt != z), zt)
            go_if(ring(d) >= FIRST, ring(d))
            go_if(ring(NZ - d) >= FIRST, ring(NZ - d))

        go_if(ring(NZ // 2) >= FIRST, ring(NZ // 2))

    def z_issue(chunk):
        s, t = chunk
        dst = rxz[s].at[t, pl.ds(z * BLK, BLK)]

        def src(zt):
            return args[t].at[:, frames_of(zt), lanes_of(zt, s)]

        def go(zt):
            pltpu.make_async_remote_copy(
                src(zt), dst, z_send.at[s, t], z_recv.at[s, t], device_id=(cam, zt * NG + g), device_id_type=MESH
            ).start()

        to_ring(go)
        pltpu.make_async_copy(src(z), dst, z_recv.at[s, t]).start()

    def wait_bytes(ref, sem):
        pltpu.make_async_copy(ref, ref, sem).wait()

    chunks = [(s, t) for s in range(len(SETS)) for t in range(3)]
    for chunk in chunks[:AHEAD]:
        z_issue(chunk)

    r = lax.broadcasted_iota(jnp.int32, (256, 256), 0)
    c = lax.broadcasted_iota(jnp.int32, (256, 256), 1)
    perm[...] = jnp.where(c == (r % 16) * 16 + r // 16, 1.0, 0.0).astype(BF)

    def column_of(idx, kind):
        room = ROOMS[kind]
        dev, k = idx // room, (idx % room) // 4
        col = jnp.full(idx.shape, -1, jnp.int32)
        for n in range(NG):
            for kk in range(COUNTS[n][kind]):
                here = jnp.logical_and(dev == n, k == kk)
                col = jnp.where(here, COLUMNS[n][sum(ROOMS[:kind]) // 4 + kk], col)
        return col

    w_right = edge_ref[cam]
    w_left = edge_ref[prior]

    def on_left(col, w):
        return jnp.logical_and(col >= 0, col < w)

    def on_right(col, w):
        return col >= COLS - w

    lane = lax.broadcasted_iota(jnp.int32, (8, NG * EDGE), 1)
    col_l, col_r = column_of(lane, 0), column_of(lane, 1)
    col_m = column_of(lax.broadcasted_iota(jnp.int32, (8, NG * MID), 1), 2)

    def as_bias(*ok):
        return jnp.concatenate([jnp.where(x, 0.0, -1e30).astype(F32) for x in ok], axis=1)

    bias[0] = as_bias(col_l >= 0, col_r >= 0, col_m >= 0)
    bias[1, :, : 2 * NG * EDGE] = as_bias(on_right(col_r, w_left), on_left(col_l, w_left))
    bias[2, :, : 2 * NG * EDGE] = as_bias(on_right(col_r, w_right), on_left(col_l, w_right))
    row = lax.broadcasted_iota(jnp.int32, (NG * EDGE, HD), 0)
    qvalid[0] = jnp.where(on_left(column_of(row, 0), w_left), 1.0, 0.0).astype(F32)
    qvalid[1] = jnp.where(on_right(column_of(row, 1), w_right), 1.0, 0.0).astype(F32)

    slot = [by_g(g, [SLOTS[n][k] for n in range(NG)]) for k in range(KINDS)]
    kinds = [(kind, k) for kind in range(3) for k in range(ROOMS[kind] // 4)]
    real = [by_g(g, [1 if k < COUNTS[n][kind] else 0 for n in range(NG)]) for kind, k in kinds]

    def place(k, a):
        if isinstance(real[k], int):
            return PER * BLK * a + slot[k]
        return jnp.where(real[k] == 1, PER * BLK * a + slot[k], POS)

    def to_frames(s, t):
        for j in range(KINDS // 4):
            x = jnp.concatenate(
                [rxz[s][t, PER * BLK * a + slot[k]] for k in range(4 * j, 4 * j + 4) for a in range(4)], axis=0
            )
            y = dot(perm[...], x, ((1,), (0,))).astype(BF)
            st2[s][t, :, 16 * j : 16 * j + 16, :] = y.reshape(FR, 16, x.shape[1])

    def to_tiles(s):
        for j in range(KINDS // 4):
            x = rxo[s][:, 16 * j : 16 * j + 16, :]
            x = x.reshape(256, x.shape[2])
            y = dot(perm[...], x, ((1,), (0,))).astype(BF).reshape(16, FR, x.shape[1])
            for n in range(16):
                otx[s][place(4 * j + n // 4, n % 4)] = y[n]

    def g_issue(s, t):
        for d in (2, 1, 3):
            gt = lax.rem(g + d, NG)
            pltpu.make_async_remote_copy(
                st2[s].at[t, pl.ds(gt * FG, FG)], rx2[s].at[t, g], g_send.at[s, t], g_recv.at[s, t],
                device_id=(cam, z * NG + gt), device_id_type=MESH,
            ).start()
        pltpu.make_async_copy(st2[s].at[t, pl.ds(g * FG, FG)], rx2[s].at[t, g], g_recv.at[s, t]).start()
        if t < 2:
            for d in range(NG):
                gt = lax.rem(g + d, NG)
                for side, who, base in ((0, after, EDGE), (1, prior, 0)):
                    pltpu.make_async_remote_copy(
                        st2[s].at[t, pl.ds(gt * FG, FG), pl.ds(base, EDGE)], edges[s].at[t, side, g],
                        e_send.at[s, t], e_recv.at[s, t],
                        device_id=(who, z * NG + gt), device_id_type=MESH,
                    ).start()

    def arrive(n):
        s, t = chunks[n]
        wait_bytes(rxz[s].at[t], z_recv.at[s, t])
        if n + AHEAD < len(chunks):
            z_issue(chunks[n + AHEAD])
        to_frames(s, t)
        g_issue(s, t)

    def weigh(q, k, v, extra):
        x = dot(q, k, ((1,), (1,))) * SCALE + extra
        p = jnp.exp2(x - jnp.max(x, axis=-1, keepdims=True))
        w = (p * (1.0 / jnp.sum(p, axis=-1, keepdims=True))).astype(BF)
        return dot(w, v, ((1,), (0,)))

    def attend(s):
        for t in range(3):
            wait_bytes(rx2[s].at[t], g_recv.at[s, t])
        for t in range(2):
            wait_bytes(edges[s].at[t], e_recv.at[s, t])
        count = SETS[s][1]

        @pl.loop(0, FG * count)
        def _(n):
            f, h = n // count, n % count
            lanes = pl.ds(pl.multiple_of(h * HD, HD), HD)

            def gather(t):
                parts, lo = [], 0
                for room in ROOMS:
                    parts.append([rx2[s][t, gs, f, lo : lo + room, lanes] for gs in range(NG)])
                    lo += room
                return [jnp.concatenate(x, axis=0) for x in parts]

            def edge(t, side):
                return jnp.concatenate([edges[s][t, side, gs, f, :, lanes] for gs in range(NG)], axis=0)

            (kl, kr, km), (vl, vr, vm), (ql, qr, qm) = gather(0), gather(1), gather(2)
            k_all, v_all = jnp.concatenate([kl, kr, km], axis=0), jnp.concatenate([vl, vr, vm], axis=0)
            k_left, v_left = jnp.concatenate([edge(0, 0), kl], axis=0), jnp.concatenate([edge(1, 0), vl], axis=0)
            k_right, v_right = jnp.concatenate([kr, edge(0, 1)], axis=0), jnp.concatenate([vr, edge(1, 1)], axis=0)
            here, joint_l, joint_r = bias[0, 0:1], bias[1, 0:1, : 2 * NG * EDGE], bias[2, 0:1, : 2 * NG * EDGE]
            o_l = weigh(ql, k_all, v_all, here) + weigh(ql, k_left, v_left, joint_l) * qvalid[0]
            o_r = weigh(qr, k_all, v_all, here) + weigh(qr, k_right, v_right, joint_r) * qvalid[1]
            o_m = weigh(qm, k_all, v_all, here)
            o_l, o_r, o_m = o_l.astype(BF), o_r.astype(BF), o_m.astype(BF)
            for gs in range(NG):
                ost[s][gs, f, 0:EDGE, lanes] = o_l[gs * EDGE : (gs + 1) * EDGE]
                ost[s][gs, f, EDGE : 2 * EDGE, lanes] = o_r[gs * EDGE : (gs + 1) * EDGE]
                ost[s][gs, f, 2 * EDGE :, lanes] = o_m[gs * MID : (gs + 1) * MID]
            for d in (2, 1, 3):
                gt = lax.rem(g + d, NG)
                pltpu.make_async_remote_copy(
                    ost[s].at[gt, f, :, lanes], rxo[s].at[g * FG + f, :, lanes], og_send.at[s], og_recv.at[s],
                    device_id=(cam, z * NG + gt), device_id_type=MESH,
                ).start()
            pltpu.make_async_copy(
                ost[s].at[g, f, :, lanes], rxo[s].at[g * FG + f, :, lanes], og_recv.at[s]
            ).start()

    def give_back(s):
        wait_bytes(rxo[s], og_recv.at[s])
        to_tiles(s)
        dst = out_ref.at[:, frames_of(z), lanes_of(z, s)]

        def go(zt):
            pltpu.make_async_remote_copy(
                otx[s].at[pl.ds(zt * BLK, BLK)], dst, oz_send.at[s], oz_recv.at[s],
                device_id=(cam, zt * NG + g), device_id_type=MESH,
            ).start()

        back_to_ring(go)
        pltpu.make_async_copy(otx[s].at[pl.ds(z * BLK, BLK)], dst, oz_recv.at[s]).start()

    arrive(0)
    arrive(1)
    arrive(2)
    arrive(3)
    attend(0)
    arrive(4)
    give_back(0)
    arrive(5)
    attend(1)
    give_back(1)

    for s in range(len(SETS)):
        for t in range(3):
            wait_bytes(rxz[s].at[t, pl.ds(0, (NZ - 1) * BLK)], z_send.at[s, t])
            wait_bytes(rx2[s].at[t, pl.ds(0, NG - 1)], g_send.at[s, t])
        for t in range(2):
            wait_bytes(edges[s].at[t], e_send.at[s, t])
        wait_bytes(ost[s].at[pl.ds(0, NG - 1)], og_send.at[s])
        wait_bytes(rxz[s].at[0, pl.ds(0, (NZ - 1) * BLK)], oz_send.at[s])
        wait_bytes(rxz[s].at[0], oz_recv.at[s])


def local(query, key, value, edge_cols):
    sems = [(2, 3)] * 4 + [(2, 2)] * 2 + [(2,)] * 4
    buffers = []
    for _, count in SETS:
        wide = count * HD
        for shape in (
            (3, POS, FR), (3, FR, ROWS_G), (3, NG, FG, ROWS_G), (2, 2, NG, FG, EDGE), (NG, FG, ROWS_G), (FR, ROWS_G), (POS + 1, FR)
        ):
            buffers.append(pltpu.VMEM(shape + (wide,), BF))
    out = pl.pallas_call(
        kernel,
        out_shape=jax.ShapeDtypeStruct(query.shape[1:], query.dtype),
        in_specs=[pl.BlockSpec(memory_space=pltpu.SMEM)] + [pl.BlockSpec(memory_space=pl.ANY)] * 3,
        out_specs=pl.BlockSpec(memory_space=pl.ANY),
        scratch_shapes=buffers
        + [pltpu.VMEM((256, 256), BF), pltpu.VMEM((3, 8, NG * ROWS_G), F32), pltpu.VMEM((2, NG * EDGE, HD), F32)]
        + [pltpu.SemaphoreType.DMA(shape) for shape in sems],
        compiler_params=pltpu.CompilerParams(collective_id=0, has_side_effects=True, vmem_limit_bytes=52 * 2**20),
    )(edge_cols, query[0], key[0], value[0])
    return out[None]


def solution(mesh):
    spec = P("cam", "seq", None, None)
    return jax.shard_map(local, mesh=mesh, in_specs=(spec, spec, spec, P()), out_specs=spec, check_vma=False)
```

```python
import jax
import jax.numpy as jnp
from jax import lax
from jax.experimental import pallas as pl
from jax.experimental.pallas import tpu as pltpu
from jax.sharding import PartitionSpec as P

MESH = pl.DeviceIdType.MESH
HD = 128
COLS = 32
MAX_COLS = 14
BF = jnp.bfloat16
F32 = jnp.float32
NZ = 16
NG = 4
BLK = 6
FR = 16
HEADS = 3
FG = 4
PER = 4
POS = NZ * BLK
EDGE = 48
MID = 16
ROWS_G = 2 * EDGE + MID
ROOMS = (EDGE, EDGE, MID)
SETS = ((0, 2), (2, 1))
AHEAD = 2
FIRST = 4
SCALE = HD**-0.5 * 1.4426950408889634


def tables():
    slots, cols, counts = [], [], []
    for g in range(NG):
        left, right, mid = [], [], []
        for b in range(PER):
            for i in range(BLK):
                col = (PER * BLK * b + BLK * g + i) % COLS
                entry = (BLK * b + i, col)
                (left if col < MAX_COLS else right if col >= COLS - MAX_COLS else mid).append(entry)
        groups = [left, right, mid]
        counts.append([len(x) for x in groups])
        row_s, row_c = [], []
        for x, room in zip(groups, [room // 4 for room in ROOMS]):
            for k in range(room):
                row_s.append(x[k][0] if k < len(x) else x[0][0])
                row_c.append(x[k][1] if k < len(x) else -1)
        slots.append(row_s)
        cols.append(row_c)
    return slots, cols, counts


SLOTS, COLUMNS, COUNTS = tables()
KINDS = len(SLOTS[0])


def by_g(g, values):
    if len(set(values)) == 1:
        return values[0]
    out = jnp.int32(values[-1])
    for n in range(len(values) - 2, -1, -1):
        out = jnp.where(g == n, jnp.int32(values[n]), out)
    return out


def dot(a, b, dims):
    return lax.dot_general(a, b, (dims, ((), ())), preferred_element_type=F32)


def kernel(
    edge_ref, q_ref, k_ref, v_ref, out_ref,
    tx_a, rkv_a, rq_a, st2_a, rx2_a, edges_a, ost_a, rxo_a, otx_a,
    tx_b, rkv_b, rq_b, st2_b, rx2_b, edges_b, ost_b, rxo_b, otx_b,
    perm, bias, qvalid,
    stage, z_send, z_recv, g_send, g_recv, e_send, e_recv, og_send, og_recv, oz_send, oz_recv,
):
    cam = lax.axis_index("cam")
    seq = lax.axis_index("seq")
    cams = lax.axis_size("cam")
    z = seq // NG
    g = seq % NG
    prior = lax.rem(cam + cams - 1, cams)
    after = lax.rem(cam + 1, cams)
    hg, fg = z // 4, z % 4
    args = (k_ref, v_ref, q_ref)
    tx, rxz = (tx_a, tx_b), ((rkv_a, rq_a), (rkv_b, rq_b))
    st2, rx2, edges = (st2_a, st2_b), (rx2_a, rx2_b), (edges_a, edges_b)
    ost, rxo, otx = (ost_a, ost_b), (rxo_a, rxo_b), (otx_a, otx_b)

    def ring(d):
        return lax.rem(z + d, NZ)

    def lanes_at(hgt, s):
        first, count = SETS[s]
        return pl.ds(pl.multiple_of((hgt * HEADS + first) * HD, HD), count * HD)

    def gather_kv(s):
        for n in range(NZ // 4):
            for t in range(2):
                pltpu.make_async_copy(args[t].at[:, :, lanes_at(n, s)], tx[s].at[n, t], stage.at[s]).start()

    gather_kv(0)

    bar = pltpu.get_barrier_semaphore()

    def greet(dev):
        pl.semaphore_signal(bar, inc=1, device_id=dev, device_id_type=MESH)

    @pl.loop(1, NZ)
    def _(d):
        greet((cam, ring(d) * NG + g))

    for d in range(1, NG):
        greet((cam, z * NG + lax.rem(g + d, NG)))
    for d in range(NG):
        greet((prior, z * NG + d))
        greet((after, z * NG + d))
    pl.semaphore_wait(bar, NZ - 1 + NG - 1 + 2 * NG)

    def lanes_of(zt, s):
        return lanes_at(zt // 4, s)

    def frames_of(zt):
        return pl.ds(pl.multiple_of((zt % 4) * FR, FR), FR)

    def to_ring(go):
        @pl.loop(1, NZ // 2)
        def _(d):
            go(ring(d))
            go(ring(NZ - d))

        go(ring(NZ // 2))

    def back_to_ring(go):
        def go_if(ok, zt):
            pl.when(ok)(lambda: go(zt))

        @pl.loop(1, NZ // 2)
        def _(d):
            zt = lax.rem(d - 1 + (g % 2) * (z + 1), FIRST)
            go_if(jnp.logical_and(d <= FIRST, zt != z), zt)
            go_if(ring(d) >= FIRST, ring(d))
            go_if(ring(NZ - d) >= FIRST, ring(NZ - d))

        go_if(ring(NZ // 2) >= FIRST, ring(NZ // 2))

    def wait_bytes(ref, sem):
        pltpu.make_async_copy(ref, ref, sem).wait()

    def z_issue(chunk):
        s, part = chunk
        dst = rxz[s][part].at[z]
        if part == 0:
            wait_bytes(tx[s], stage.at[s])

        def src(zt):
            if part == 0:
                return tx[s].at[zt // 4, :, :, frames_of(zt)]
            return q_ref.at[:, frames_of(zt), lanes_of(zt, s)]

        def go(zt):
            pltpu.make_async_remote_copy(
                src(zt), dst, z_send.at[s, part], z_recv.at[s, part],
                device_id=(cam, zt * NG + g), device_id_type=MESH,
            ).start()

        to_ring(go)
        pltpu.make_async_copy(src(z), dst, z_recv.at[s, part]).start()

    chunks = [(s, part) for s in range(len(SETS)) for part in range(2)]
    for chunk in chunks[:AHEAD]:
        z_issue(chunk)
    gather_kv(1)

    r = lax.broadcasted_iota(jnp.int32, (256, 256), 0)
    c = lax.broadcasted_iota(jnp.int32, (256, 256), 1)
    perm[...] = jnp.where(c == (r % 16) * 16 + r // 16, 1.0, 0.0).astype(BF)

    def column_of(idx, kind):
        room = ROOMS[kind]
        dev, k = idx // room, (idx % room) // 4
        col = jnp.full(idx.shape, -1, jnp.int32)
        for n in range(NG):
            for kk in range(COUNTS[n][kind]):
                here = jnp.logical_and(dev == n, k == kk)
                col = jnp.where(here, COLUMNS[n][sum(ROOMS[:kind]) // 4 + kk], col)
        return col

    w_right = edge_ref[cam]
    w_left = edge_ref[prior]

    def on_left(col, w):
        return jnp.logical_and(col >= 0, col < w)

    def on_right(col, w):
        return col >= COLS - w

    lane = lax.broadcasted_iota(jnp.int32, (8, NG * EDGE), 1)
    col_l, col_r = column_of(lane, 0), column_of(lane, 1)
    col_m = column_of(lax.broadcasted_iota(jnp.int32, (8, NG * MID), 1), 2)

    def as_bias(*ok):
        return jnp.concatenate([jnp.where(x, 0.0, -1e30).astype(F32) for x in ok], axis=1)

    bias[0] = as_bias(col_l >= 0, col_r >= 0, col_m >= 0)
    bias[1, :, : 2 * NG * EDGE] = as_bias(on_right(col_r, w_left), on_left(col_l, w_left))
    bias[2, :, : 2 * NG * EDGE] = as_bias(on_right(col_r, w_right), on_left(col_l, w_right))
    row = lax.broadcasted_iota(jnp.int32, (NG * EDGE, HD), 0)
    qvalid[0] = jnp.where(on_left(column_of(row, 0), w_left), 1.0, 0.0).astype(F32)
    qvalid[1] = jnp.where(on_right(column_of(row, 1), w_right), 1.0, 0.0).astype(F32)

    slot = [by_g(g, [SLOTS[n][k] for n in range(NG)]) for k in range(KINDS)]
    slot_z = [by_g(g, [SLOTS[n][k] // BLK for n in range(NG)]) for k in range(KINDS)]
    slot_i = [by_g(g, [SLOTS[n][k] % BLK for n in range(NG)]) for k in range(KINDS)]
    kinds = [(kind, k) for kind in range(3) for k in range(ROOMS[kind] // 4)]
    real = [by_g(g, [1 if k < COUNTS[n][kind] else 0 for n in range(NG)]) for kind, k in kinds]

    def place(k, a):
        if isinstance(real[k], int):
            return PER * BLK * a + slot[k]
        return jnp.where(real[k] == 1, PER * BLK * a + slot[k], POS)

    def to_frames(s, t):
        for j in range(KINDS // 4):
            tiles = []
            for k in range(4 * j, 4 * j + 4):
                for a in range(4):
                    where = (PER * a + slot_z[k], slot_i[k])
                    tiles.append(rxz[s][1][where] if t == 2 else rxz[s][0][where[0], t, where[1]])
            x = jnp.concatenate(tiles, axis=0)
            y = dot(perm[...], x, ((1,), (0,))).astype(BF)
            st2[s][t, :, 16 * j : 16 * j + 16, :] = y.reshape(FR, 16, x.shape[1])

    def to_tiles(s):
        for j in range(KINDS // 4):
            x = rxo[s][:, 16 * j : 16 * j + 16, :]
            x = x.reshape(256, x.shape[2])
            y = dot(perm[...], x, ((1,), (0,))).astype(BF).reshape(16, FR, x.shape[1])
            for n in range(16):
                otx[s][place(4 * j + n // 4, n % 4)] = y[n]

    def g_issue(s, t):
        for d in (2, 1, 3):
            gt = lax.rem(g + d, NG)
            pltpu.make_async_remote_copy(
                st2[s].at[t, pl.ds(gt * FG, FG)], rx2[s].at[t, g], g_send.at[s, t], g_recv.at[s, t],
                device_id=(cam, z * NG + gt), device_id_type=MESH,
            ).start()
        pltpu.make_async_copy(st2[s].at[t, pl.ds(g * FG, FG)], rx2[s].at[t, g], g_recv.at[s, t]).start()
        if t < 2:
            for d in range(NG):
                gt = lax.rem(g + d, NG)
                for side, who, base in ((0, after, EDGE), (1, prior, 0)):
                    pltpu.make_async_remote_copy(
                        st2[s].at[t, pl.ds(gt * FG, FG), pl.ds(base, EDGE)], edges[s].at[t, side, g],
                        e_send.at[s, t], e_recv.at[s, t],
                        device_id=(who, z * NG + gt), device_id_type=MESH,
                    ).start()

    def arrive(n):
        s, part = chunks[n]
        wait_bytes(rxz[s][part], z_recv.at[s, part])
        if n + AHEAD < len(chunks):
            z_issue(chunks[n + AHEAD])
        for t in ((0, 1), (2,))[part]:
            to_frames(s, t)
            g_issue(s, t)

    def weigh(q, k, v, extra):
        x = dot(q, k, ((1,), (1,))) * SCALE + extra
        p = jnp.exp2(x - jnp.max(x, axis=-1, keepdims=True))
        w = (p * (1.0 / jnp.sum(p, axis=-1, keepdims=True))).astype(BF)
        return dot(w, v, ((1,), (0,)))

    def attend(s):
        for t in range(3):
            wait_bytes(rx2[s].at[t], g_recv.at[s, t])
        for t in range(2):
            wait_bytes(edges[s].at[t], e_recv.at[s, t])
        count = SETS[s][1]

        @pl.loop(0, FG * count)
        def _(n):
            f, h = n // count, n % count
            lanes = pl.ds(pl.multiple_of(h * HD, HD), HD)

            def gather(t):
                parts, lo = [], 0
                for room in ROOMS:
                    parts.append([rx2[s][t, gs, f, lo : lo + room, lanes] for gs in range(NG)])
                    lo += room
                return [jnp.concatenate(x, axis=0) for x in parts]

            def edge(t, side):
                return jnp.concatenate([edges[s][t, side, gs, f, :, lanes] for gs in range(NG)], axis=0)

            (kl, kr, km), (vl, vr, vm), (ql, qr, qm) = gather(0), gather(1), gather(2)
            k_all, v_all = jnp.concatenate([kl, kr, km], axis=0), jnp.concatenate([vl, vr, vm], axis=0)
            k_left, v_left = jnp.concatenate([edge(0, 0), kl], axis=0), jnp.concatenate([edge(1, 0), vl], axis=0)
            k_right, v_right = jnp.concatenate([kr, edge(0, 1)], axis=0), jnp.concatenate([vr, edge(1, 1)], axis=0)
            here, joint_l, joint_r = bias[0, 0:1], bias[1, 0:1, : 2 * NG * EDGE], bias[2, 0:1, : 2 * NG * EDGE]
            o_l = weigh(ql, k_all, v_all, here) + weigh(ql, k_left, v_left, joint_l) * qvalid[0]
            o_r = weigh(qr, k_all, v_all, here) + weigh(qr, k_right, v_right, joint_r) * qvalid[1]
            o_m = weigh(qm, k_all, v_all, here)
            o_l, o_r, o_m = o_l.astype(BF), o_r.astype(BF), o_m.astype(BF)
            for gs in range(NG):
                ost[s][gs, f, 0:EDGE, lanes] = o_l[gs * EDGE : (gs + 1) * EDGE]
                ost[s][gs, f, EDGE : 2 * EDGE, lanes] = o_r[gs * EDGE : (gs + 1) * EDGE]
                ost[s][gs, f, 2 * EDGE :, lanes] = o_m[gs * MID : (gs + 1) * MID]
            for d in (2, 1, 3):
                gt = lax.rem(g + d, NG)
                pltpu.make_async_remote_copy(
                    ost[s].at[gt, f, :, lanes], rxo[s].at[g * FG + f, :, lanes], og_send.at[s], og_recv.at[s],
                    device_id=(cam, z * NG + gt), device_id_type=MESH,
                ).start()
            pltpu.make_async_copy(
                ost[s].at[g, f, :, lanes], rxo[s].at[g * FG + f, :, lanes], og_recv.at[s]
            ).start()

    def give_back(s):
        wait_bytes(rxo[s], og_recv.at[s])
        to_tiles(s)
        dst = out_ref.at[:, frames_of(z), lanes_of(z, s)]

        def go(zt):
            pltpu.make_async_remote_copy(
                otx[s].at[pl.ds(zt * BLK, BLK)], dst, oz_send.at[s], oz_recv.at[s],
                device_id=(cam, zt * NG + g), device_id_type=MESH,
            ).start()

        back_to_ring(go)
        pltpu.make_async_copy(otx[s].at[pl.ds(z * BLK, BLK)], dst, oz_recv.at[s]).start()

    arrive(0)
    arrive(1)
    attend(0)
    arrive(2)
    give_back(0)
    arrive(3)
    attend(1)
    give_back(1)

    for s in range(len(SETS)):
        for t in range(3):
            wait_bytes(rx2[s].at[t, pl.ds(0, NG - 1)], g_send.at[s, t])
        for t in range(2):
            wait_bytes(edges[s].at[t], e_send.at[s, t])
        wait_bytes(ost[s].at[pl.ds(0, NG - 1)], og_send.at[s])
        for part in range(2):
            wait_bytes(rxz[s][part].at[pl.ds(0, NZ - 1)], z_send.at[s, part])
        wait_bytes(rxz[s][1].at[pl.ds(0, NZ - 1)], oz_send.at[s])
        wait_bytes(rxz[s][1], oz_recv.at[s])


def local(query, key, value, edge_cols):
    sems = [(2,)] + [(2, 2)] * 2 + [(2, 3)] * 2 + [(2, 2)] * 2 + [(2,)] * 4
    buffers = []
    for _, count in SETS:
        wide = count * HD
        for shape in (
            (NZ // 4, 2, BLK, query.shape[2]), (NZ, 2, BLK, FR), (NZ, BLK, FR), (3, FR, ROWS_G), (3, NG, FG, ROWS_G), (2, 2, NG, FG, EDGE), (NG, FG, ROWS_G), (FR, ROWS_G), (POS + 1, FR)
        ):
            buffers.append(pltpu.VMEM(shape + (wide,), BF))
    out = pl.pallas_call(
        kernel,
        out_shape=jax.ShapeDtypeStruct(query.shape[1:], query.dtype),
        in_specs=[pl.BlockSpec(memory_space=pltpu.SMEM)] + [pl.BlockSpec(memory_space=pl.ANY)] * 3,
        out_specs=pl.BlockSpec(memory_space=pl.ANY),
        scratch_shapes=buffers
        + [pltpu.VMEM((256, 256), BF), pltpu.VMEM((3, 8, NG * ROWS_G), F32), pltpu.VMEM((2, NG * EDGE, HD), F32)]
        + [pltpu.SemaphoreType.DMA(shape) for shape in sems],
        compiler_params=pltpu.CompilerParams(collective_id=0, has_side_effects=True, vmem_limit_bytes=52 * 2**20),
    )(edge_cols, query[0], key[0], value[0])
    return out[None]


def solution(mesh):
    spec = P("cam", "seq", None, None)
    return jax.shard_map(local, mesh=mesh, in_specs=(spec, spec, spec, P()), out_specs=spec, check_vma=False)
```

```python
import jax
import jax.numpy as jnp
from jax import lax
from jax.experimental import pallas as pl
from jax.experimental.pallas import tpu as pltpu
from jax.sharding import PartitionSpec as P

MESH = pl.DeviceIdType.MESH
HD = 128
COLS = 32
MAX_COLS = 14
BF = jnp.bfloat16
F32 = jnp.float32
NZ = 16
NG = 4
BLK = 6
FR = 16
HEADS = 3
FG = 4
PER = 4
POS = NZ * BLK
EDGE = 48
MID = 16
ROWS_G = 2 * EDGE + MID
ROOMS = (EDGE, EDGE, MID)
SETS = ((0, 2), (2, 1))
AHEAD = 2
FIRST = 4
SCALE = HD**-0.5 * 1.4426950408889634


def tables():
    slots, cols, counts = [], [], []
    for g in range(NG):
        left, right, mid = [], [], []
        for b in range(PER):
            for i in range(BLK):
                col = (PER * BLK * b + BLK * g + i) % COLS
                entry = (BLK * b + i, col)
                (left if col < MAX_COLS else right if col >= COLS - MAX_COLS else mid).append(entry)
        groups = [left, right, mid]
        counts.append([len(x) for x in groups])
        row_s, row_c = [], []
        for x, room in zip(groups, [room // 4 for room in ROOMS]):
            for k in range(room):
                row_s.append(x[k][0] if k < len(x) else x[0][0])
                row_c.append(x[k][1] if k < len(x) else -1)
        slots.append(row_s)
        cols.append(row_c)
    return slots, cols, counts


SLOTS, COLUMNS, COUNTS = tables()
KINDS = len(SLOTS[0])


def by_g(g, values):
    if len(set(values)) == 1:
        return values[0]
    out = jnp.int32(values[-1])
    for n in range(len(values) - 2, -1, -1):
        out = jnp.where(g == n, jnp.int32(values[n]), out)
    return out


def dot(a, b, dims):
    return lax.dot_general(a, b, (dims, ((), ())), preferred_element_type=F32)


def kernel(
    edge_ref, q_ref, k_ref, v_ref, out_ref,
    tx_a, rkv_a, rq_a, st2_a, rx2_a, edges_a, ost_a, rxo_a, otx_a,
    tx_b, rkv_b, rq_b, st2_b, rx2_b, edges_b, ost_b, rxo_b, otx_b,
    perm, bias, qvalid,
    stage, z_send, z_recv, g_send, g_recv, e_send, e_recv, og_send, og_recv, oz_send, oz_recv,
):
    cam = lax.axis_index("cam")
    seq = lax.axis_index("seq")
    cams = lax.axis_size("cam")
    z = seq // NG
    g = seq % NG
    prior = lax.rem(cam + cams - 1, cams)
    after = lax.rem(cam + 1, cams)
    hg, fg = z // 4, z % 4
    args = (k_ref, v_ref, q_ref)
    tx, rxz = (tx_a, tx_b), ((rkv_a, rq_a), (rkv_b, rq_b))
    st2, rx2, edges = (st2_a, st2_b), (rx2_a, rx2_b), (edges_a, edges_b)
    ost, rxo, otx = (ost_a, ost_b), (rxo_a, rxo_b), (otx_a, otx_b)

    def ring(d):
        return lax.rem(z + d, NZ)

    def lanes_at(hgt, s):
        first, count = SETS[s]
        return pl.ds(pl.multiple_of((hgt * HEADS + first) * HD, HD), count * HD)

    def gather_kv(s):
        for n in range(NZ // 4):
            for t in range(2):
                pltpu.make_async_copy(args[t].at[:, :, lanes_at(n, s)], tx[s].at[n, t], stage.at[s]).start()

    bar = pltpu.get_barrier_semaphore()

    def greet(dev):
        pl.semaphore_signal(bar, inc=1, device_id=dev, device_id_type=MESH)

    @pl.loop(1, NZ)
    def _(d):
        greet((cam, ring(d) * NG + g))

    for d in range(1, NG):
        greet((cam, z * NG + lax.rem(g + d, NG)))
    for d in range(NG):
        greet((prior, z * NG + d))
        greet((after, z * NG + d))
    gather_kv(0)
    pl.semaphore_wait(bar, NZ - 1 + NG - 1 + 2 * NG)

    def lanes_of(zt, s):
        return lanes_at(zt // 4, s)

    def frames_of(zt):
        return pl.ds(pl.multiple_of((zt % 4) * FR, FR), FR)

    def to_ring(go):
        @pl.loop(1, NZ // 2)
        def _(d):
            go(ring(d))
            go(ring(NZ - d))

        go(ring(NZ // 2))

    def back_to_ring(go):
        def go_if(ok, zt):
            pl.when(ok)(lambda: go(zt))

        @pl.loop(1, NZ // 2)
        def _(d):
            zt = lax.rem(d - 1 + (g % 2) * (z + 1), FIRST)
            go_if(jnp.logical_and(d <= FIRST, zt != z), zt)
            go_if(ring(d) >= FIRST, ring(d))
            go_if(ring(NZ - d) >= FIRST, ring(NZ - d))

        go_if(ring(NZ // 2) >= FIRST, ring(NZ // 2))

    def wait_bytes(ref, sem):
        pltpu.make_async_copy(ref, ref, sem).wait()

    def z_issue(chunk):
        s, part = chunk
        dst = rxz[s][part].at[z]
        if part == 0:
            wait_bytes(tx[s], stage.at[s])

        def src(zt):
            if part == 0:
                return tx[s].at[zt // 4, :, :, frames_of(zt)]
            return q_ref.at[:, frames_of(zt), lanes_of(zt, s)]

        def go(zt):
            pltpu.make_async_remote_copy(
                src(zt), dst, z_send.at[s, part], z_recv.at[s, part],
                device_id=(cam, zt * NG + g), device_id_type=MESH,
            ).start()

        to_ring(go)
        pltpu.make_async_copy(src(z), dst, z_recv.at[s, part]).start()

    chunks = [(s, part) for s in range(len(SETS)) for part in range(2)]
    for chunk in chunks[:AHEAD]:
        z_issue(chunk)
    gather_kv(1)

    r = lax.broadcasted_iota(jnp.int32, (256, 256), 0)
    c = lax.broadcasted_iota(jnp.int32, (256, 256), 1)
    perm[...] = jnp.where(c == (r % 16) * 16 + r // 16, 1.0, 0.0).astype(BF)

    def column_of(idx, kind):
        room = ROOMS[kind]
        dev, k = idx // room, (idx % room) // 4
        col = jnp.full(idx.shape, -1, jnp.int32)
        for n in range(NG):
            for kk in range(COUNTS[n][kind]):
                here = jnp.logical_and(dev == n, k == kk)
                col = jnp.where(here, COLUMNS[n][sum(ROOMS[:kind]) // 4 + kk], col)
        return col

    w_right = edge_ref[cam]
    w_left = edge_ref[prior]

    def on_left(col, w):
        return jnp.logical_and(col >= 0, col < w)

    def on_right(col, w):
        return col >= COLS - w

    lane = lax.broadcasted_iota(jnp.int32, (8, NG * EDGE), 1)
    col_l, col_r = column_of(lane, 0), column_of(lane, 1)
    col_m = column_of(lax.broadcasted_iota(jnp.int32, (8, NG * MID), 1), 2)

    def as_bias(*ok):
        return jnp.concatenate([jnp.where(x, 0.0, -1e30).astype(F32) for x in ok], axis=1)

    bias[0] = as_bias(col_l >= 0, col_r >= 0, col_m >= 0)
    bias[1, :, : 2 * NG * EDGE] = as_bias(on_right(col_r, w_left), on_left(col_l, w_left))
    bias[2, :, : 2 * NG * EDGE] = as_bias(on_right(col_r, w_right), on_left(col_l, w_right))
    row = lax.broadcasted_iota(jnp.int32, (NG * EDGE, HD), 0)
    qvalid[0] = jnp.where(on_left(column_of(row, 0), w_left), 1.0, 0.0).astype(F32)
    qvalid[1] = jnp.where(on_right(column_of(row, 1), w_right), 1.0, 0.0).astype(F32)

    slot = [by_g(g, [SLOTS[n][k] for n in range(NG)]) for k in range(KINDS)]
    slot_z = [by_g(g, [SLOTS[n][k] // BLK for n in range(NG)]) for k in range(KINDS)]
    slot_i = [by_g(g, [SLOTS[n][k] % BLK for n in range(NG)]) for k in range(KINDS)]
    kinds = [(kind, k) for kind in range(3) for k in range(ROOMS[kind] // 4)]
    real = [by_g(g, [1 if k < COUNTS[n][kind] else 0 for n in range(NG)]) for kind, k in kinds]

    def place(k, a):
        if isinstance(real[k], int):
            return PER * BLK * a + slot[k]
        return jnp.where(real[k] == 1, PER * BLK * a + slot[k], POS)

    def to_frames(s, t):
        for j in range(KINDS // 4):
            tiles = []
            for k in range(4 * j, 4 * j + 4):
                for a in range(4):
                    where = (PER * a + slot_z[k], slot_i[k])
                    tiles.append(rxz[s][1][where] if t == 2 else rxz[s][0][where[0], t, where[1]])
            x = jnp.concatenate(tiles, axis=0)
            y = dot(perm[...], x, ((1,), (0,))).astype(BF)
            st2[s][t, :, 16 * j : 16 * j + 16, :] = y.reshape(FR, 16, x.shape[1])

    def to_tiles(s):
        for j in range(KINDS // 4):
            x = rxo[s][:, 16 * j : 16 * j + 16, :]
            x = x.reshape(256, x.shape[2])
            y = dot(perm[...], x, ((1,), (0,))).astype(BF).reshape(16, FR, x.shape[1])
            for n in range(16):
                otx[s][place(4 * j + n // 4, n % 4)] = y[n]

    def g_issue(s, t):
        for d in (2, 1, 3):
            gt = lax.rem(g + d, NG)
            pltpu.make_async_remote_copy(
                st2[s].at[t, pl.ds(gt * FG, FG)], rx2[s].at[t, g], g_send.at[s, t], g_recv.at[s, t],
                device_id=(cam, z * NG + gt), device_id_type=MESH,
            ).start()
        pltpu.make_async_copy(st2[s].at[t, pl.ds(g * FG, FG)], rx2[s].at[t, g], g_recv.at[s, t]).start()
        if t < 2:
            for d in range(NG):
                gt = lax.rem(g + d, NG)
                for side, who, base in ((0, after, EDGE), (1, prior, 0)):
                    pltpu.make_async_remote_copy(
                        st2[s].at[t, pl.ds(gt * FG, FG), pl.ds(base, EDGE)], edges[s].at[t, side, g],
                        e_send.at[s, t], e_recv.at[s, t],
                        device_id=(who, z * NG + gt), device_id_type=MESH,
                    ).start()

    def arrive(n):
        s, part = chunks[n]
        wait_bytes(rxz[s][part], z_recv.at[s, part])
        if n + AHEAD < len(chunks):
            z_issue(chunks[n + AHEAD])
        for t in ((0, 1), (2,))[part]:
            to_frames(s, t)
            g_issue(s, t)

    def weigh(q, k, v, extra):
        x = dot(q, k, ((1,), (1,))) * SCALE + extra
        p = jnp.exp2(x - jnp.max(x, axis=-1, keepdims=True))
        w = (p * (1.0 / jnp.sum(p, axis=-1, keepdims=True))).astype(BF)
        return dot(w, v, ((1,), (0,)))

    def attend(s):
        for t in range(3):
            wait_bytes(rx2[s].at[t], g_recv.at[s, t])
        for t in range(2):
            wait_bytes(edges[s].at[t], e_recv.at[s, t])
        count = SETS[s][1]

        @pl.loop(0, FG * count)
        def _(n):
            f, h = n // count, n % count
            lanes = pl.ds(pl.multiple_of(h * HD, HD), HD)

            def gather(t):
                parts, lo = [], 0
                for room in ROOMS:
                    parts.append([rx2[s][t, gs, f, lo : lo + room, lanes] for gs in range(NG)])
                    lo += room
                return [jnp.concatenate(x, axis=0) for x in parts]

            def edge(t, side):
                return jnp.concatenate([edges[s][t, side, gs, f, :, lanes] for gs in range(NG)], axis=0)

            (kl, kr, km), (vl, vr, vm), (ql, qr, qm) = gather(0), gather(1), gather(2)
            k_all, v_all = jnp.concatenate([kl, kr, km], axis=0), jnp.concatenate([vl, vr, vm], axis=0)
            k_left, v_left = jnp.concatenate([edge(0, 0), kl], axis=0), jnp.concatenate([edge(1, 0), vl], axis=0)
            k_right, v_right = jnp.concatenate([kr, edge(0, 1)], axis=0), jnp.concatenate([vr, edge(1, 1)], axis=0)
            here, joint_l, joint_r = bias[0, 0:1], bias[1, 0:1, : 2 * NG * EDGE], bias[2, 0:1, : 2 * NG * EDGE]
            o_l = weigh(ql, k_all, v_all, here) + weigh(ql, k_left, v_left, joint_l) * qvalid[0]
            o_r = weigh(qr, k_all, v_all, here) + weigh(qr, k_right, v_right, joint_r) * qvalid[1]
            o_m = weigh(qm, k_all, v_all, here)
            o_l, o_r, o_m = o_l.astype(BF), o_r.astype(BF), o_m.astype(BF)
            for gs in range(NG):
                ost[s][gs, f, 0:EDGE, lanes] = o_l[gs * EDGE : (gs + 1) * EDGE]
                ost[s][gs, f, EDGE : 2 * EDGE, lanes] = o_r[gs * EDGE : (gs + 1) * EDGE]
                ost[s][gs, f, 2 * EDGE :, lanes] = o_m[gs * MID : (gs + 1) * MID]
            for d in (2, 1, 3):
                gt = lax.rem(g + d, NG)
                pltpu.make_async_remote_copy(
                    ost[s].at[gt, f, :, lanes], rxo[s].at[g * FG + f, :, lanes], og_send.at[s], og_recv.at[s],
                    device_id=(cam, z * NG + gt), device_id_type=MESH,
                ).start()
            pltpu.make_async_copy(
                ost[s].at[g, f, :, lanes], rxo[s].at[g * FG + f, :, lanes], og_recv.at[s]
            ).start()

    def give_back(s):
        wait_bytes(rxo[s], og_recv.at[s])
        to_tiles(s)
        dst = out_ref.at[:, frames_of(z), lanes_of(z, s)]

        def go(zt):
            pltpu.make_async_remote_copy(
                otx[s].at[pl.ds(zt * BLK, BLK)], dst, oz_send.at[s], oz_recv.at[s],
                device_id=(cam, zt * NG + g), device_id_type=MESH,
            ).start()

        back_to_ring(go)
        pltpu.make_async_copy(otx[s].at[pl.ds(z * BLK, BLK)], dst, oz_recv.at[s]).start()

    arrive(0)
    arrive(1)
    attend(0)
    arrive(2)
    give_back(0)
    arrive(3)
    attend(1)
    give_back(1)

    for s in range(len(SETS)):
        for t in range(3):
            wait_bytes(rx2[s].at[t, pl.ds(0, NG - 1)], g_send.at[s, t])
        for t in range(2):
            wait_bytes(edges[s].at[t], e_send.at[s, t])
        wait_bytes(ost[s].at[pl.ds(0, NG - 1)], og_send.at[s])
        for part in range(2):
            wait_bytes(rxz[s][part].at[pl.ds(0, NZ - 1)], z_send.at[s, part])
        wait_bytes(rxz[s][1].at[pl.ds(0, NZ - 1)], oz_send.at[s])
        wait_bytes(rxz[s][1], oz_recv.at[s])


def local(query, key, value, edge_cols):
    sems = [(2,)] + [(2, 2)] * 2 + [(2, 3)] * 2 + [(2, 2)] * 2 + [(2,)] * 4
    buffers = []
    for _, count in SETS:
        wide = count * HD
        for shape in (
            (NZ // 4, 2, BLK, query.shape[2]), (NZ, 2, BLK, FR), (NZ, BLK, FR), (3, FR, ROWS_G), (3, NG, FG, ROWS_G), (2, 2, NG, FG, EDGE), (NG, FG, ROWS_G), (FR, ROWS_G), (POS + 1, FR)
        ):
            buffers.append(pltpu.VMEM(shape + (wide,), BF))
    out = pl.pallas_call(
        kernel,
        out_shape=jax.ShapeDtypeStruct(query.shape[1:], query.dtype),
        in_specs=[pl.BlockSpec(memory_space=pltpu.SMEM)] + [pl.BlockSpec(memory_space=pl.ANY)] * 3,
        out_specs=pl.BlockSpec(memory_space=pl.ANY),
        scratch_shapes=buffers
        + [pltpu.VMEM((256, 256), BF), pltpu.VMEM((3, 8, NG * ROWS_G), F32), pltpu.VMEM((2, NG * EDGE, HD), F32)]
        + [pltpu.SemaphoreType.DMA(shape) for shape in sems],
        compiler_params=pltpu.CompilerParams(collective_id=0, has_side_effects=True, vmem_limit_bytes=52 * 2**20),
    )(edge_cols, query[0], key[0], value[0])
    return out[None]


def solution(mesh):
    spec = P("cam", "seq", None, None)
    return jax.shard_map(local, mesh=mesh, in_specs=(spec, spec, spec, P()), out_specs=spec, check_vma=False)
```
